32 devices in a mesh: seq: 8 (over z, y), shard: 4 (over x, core).
Axes of the slice: x: 2, y: 2, z: 4, core: 2. Of those that a mesh axis runs over, the one named last changes fastest.
Arguments:
- block_input: bfloat16 [8, 4096, 640], P('shard', 'seq'), may hold values from -6 to 6
- out_grad: bfloat16 [8, 4096, 640], P('shard', 'seq'), may hold values from -6 to 6
- positions: int32 [8, 4096], P('shard', 'seq'), may hold values from 0 to 6142, as said below
- segments: int32 [8, 4096], P('shard', 'seq'), may hold values from 0 to 4, as said below
- qkv_weight: float32 [640, 1536], P(None, 'shard'), may hold values from -0.25 to 0.25
- out_weight: float32 [1024, 640], P('shard'), may hold values from -0.1875 to 0.1875
- ff_in_weight: float32 [2, 640, 2048], P(None, None, 'shard'), may hold values from -0.25 to 0.25
- ff_out_weight: float32 [2048, 640], P('shard'), may hold values from -0.125 to 0.125
- norm_gains: float32 [3072], P('shard'), may hold values from 0.5 to 1.5
- qkv_moment: float32 [640, 1536], P(None, 'shard'), as said below
- qkv_square: float32 [640, 1536], P(None, 'shard'), may hold values from 1724 to 6898
- out_moment: float32 [1024, 640], P('shard'), as said below
- out_square: float32 [1024, 640], P('shard'), may hold values from 1724 to 6898
- ff_in_moment: float32 [2, 640, 2048], P(None, None, 'shard'), as said below
- ff_in_square: float32 [2, 640, 2048], P(None, None, 'shard'), may hold values from 1724 to 6898
- ff_out_moment: float32 [2048, 640], P('shard'), as said below
- ff_out_square: float32 [2048, 640], P('shard'), may hold values from 1724 to 6898
- gains_moment: float32 [3072], P('shard'), as said below
- gains_square: float32 [3072], P('shard'), may hold values from 1724 to 6898
Outputs:
- mixed: bfloat16 [8, 4096, 640], P('shard', 'seq')
- input_grad: bfloat16 [8, 4096, 640], P('shard', 'seq')
- qkv_updated: float32 [640, 1536], P(None, 'shard')
- qkv_moment_new: float32 [640, 1536], P(None, 'shard')
- qkv_square_new: float32 [640, 1536], P(None, 'shard')
- out_updated: float32 [1024, 640], P('shard')
- out_moment_new: float32 [1024, 640], P('shard')
- out_square_new: float32 [1024, 640], P('shard')
- ff_in_updated: float32 [2, 640, 2048], P(None, None, 'shard')
- ff_in_moment_new: float32 [2, 640, 2048], P(None, None, 'shard')
- ff_in_square_new: float32 [2, 640, 2048], P(None, None, 'shard')
- ff_out_updated: float32 [2048, 640], P('shard')
- ff_out_moment_new: float32 [2048, 640], P('shard')
- ff_out_square_new: float32 [2048, 640], P('shard')
- gains_updated: float32 [3072], P('shard')
- gains_moment_new: float32 [3072], P('shard')
- gains_square_new: float32 [3072], P('shard')
The draws below stay inside these ranges and needn't reach their ends.
Inputs may be any that keep to these rules, and one draw needn't show every extreme that they name: `segments`: within each sequence the ids start at 0 and never fall; in each aligned group of 2 sequences one sequence is a single document, and every other sequence has exactly 5 documents. `positions`: A token's position is its document's first position plus its distance from the document's first token; each document's first position is below 2048. `qkv_moment`: entries of mean zero with a deviation of 0.111 times the square root of 32768. `out_moment`: entries of mean zero with a deviation of 0.111 times the square root of 32768. `ff_in_moment`: entries of mean zero with a deviation of 0.111 times the square root of 32768. `ff_out_moment`: entries of mean zero with a deviation of 0.111 times the square root of 32768. `gains_moment`: entries of mean zero with a deviation of 0.111 times the square root of 32768.
All inputs are finite; a program needn't handle non-finite values.
Results may differ from the reference program's by a relative error of at most 0.02.
The reference program's roundings to bfloat16 on the way count: a program that leaves them out, or rounds other values in their place, can miss the bound.
Values may be sent and summed in bfloat16 or wider, within the bound.
A program may use at most 192 MiB of HBM per device.

```python
import math
from functools import partial
import jax
import jax.numpy as jnp
from jax import lax

D = 640
QH = 4
HEAD = 256
FF = 2048
WINDOW = 512
SPAN = 512
SEQ_DEV = 2
STEP = 10
LEN = 4096
SEQS = 8
TOKENS = 32768
GAINS = 3072
N_SHARD = 4


def document_layout(key):
    key_breaks, key_whole, key_offsets = jax.random.split(key, 3)
    token_index = jnp.arange(LEN, dtype=jnp.int32)
    break_count = max(LEN // (2 * SPAN), 1)
    row_keys = jax.random.split(key_breaks, SEQS)

    def row_breaks(row_key):
        chosen_places = jax.random.permutation(row_key, LEN - 1)[:break_count] + 1
        return jnp.zeros((LEN,), jnp.int32).at[chosen_places].set(1) > 0
    breaks = jax.vmap(row_breaks)(row_keys)
    chosen = jax.random.randint(key_whole, (N_SHARD,), 0, SEQ_DEV)
    seq_rows = jnp.arange(SEQS, dtype=jnp.int32)
    group_rows = seq_rows // SEQ_DEV
    single = seq_rows % SEQ_DEV == chosen[group_rows]
    breaks = breaks & jnp.logical_not(single)[:, None]
    segments = jnp.cumsum(breaks.astype(jnp.int32), axis=1).astype(jnp.int32)
    starts = lax.cummax(jnp.where(breaks, token_index[None, :], 0), axis=1)
    offsets = jax.random.randint(key_offsets, (SEQS, LEN), 0, 2048)
    single_offset = jnp.where(group_rows == 0, 0, 2047).astype(jnp.int32)
    offsets = jnp.where(single[:, None], single_offset[:, None], offsets)
    firsts = jnp.take_along_axis(offsets, segments, axis=1)
    return (segments, (firsts + token_index[None, :] - starts).astype(jnp.int32))


def draw_positions(key, part):
    return document_layout(key)[1]


def draw_segments(key, part):
    return document_layout(key)[0]


def moment_draw(key, array_shape):
    return jax.random.normal(key, array_shape, jnp.float32) * TOKENS ** 0.5 * 0.111


def draw_qkv_moment(key, part):
    key = jax.random.fold_in(key, 11)
    return moment_draw(key, (D, (QH + 2) * HEAD))


def draw_out_moment(key, part):
    key = jax.random.fold_in(key, 12)
    return moment_draw(key, (QH * HEAD, D))


def draw_ff_in_moment(key, part):
    key = jax.random.fold_in(key, 13)
    return moment_draw(key, (2, D, FF))


def draw_ff_out_moment(key, part):
    key = jax.random.fold_in(key, 14)
    return moment_draw(key, (FF, D))


def draw_gains_moment(key, part):
    key = jax.random.fold_in(key, 15)
    return moment_draw(key, (GAINS,))


def steps_of(stream_key, dims, shards, smallest, top_value):
    gain, own = 1.0, jax.random.fold_in(stream_key, 6)
    for axis_at, parts in shards:
        heights = jnp.exp(jax.random.uniform(jax.random.fold_in(own, axis_at), (parts,), jnp.float32, smallest / len(shards), top_value / len(shards)))
        gain = gain * jnp.repeat(heights, dims[axis_at] // parts).reshape([-1 if axis == axis_at else 1 for axis in range(len(dims))])
    return gain


def normal_values(rng, extent, width, most, shards=(), kind=jnp.bfloat16):
    factor_of = steps_of(rng, extent, shards, -0.22, 0.18) if shards else 1.0
    entries = jax.random.normal(rng, extent, jnp.float32) * width * factor_of
    return jnp.minimum(jnp.maximum(entries, -most), most).astype(kind)


def setup_inputs(seed: int = 0) -> dict:
    key_of = jax.random.split(jax.random.key(seed), 20)
    return {
        "block_input": normal_values(key_of[0], (SEQS, LEN, D), 1.0, 6.0, ((0, 4), (1, 8))),
        "out_grad": normal_values(key_of[1], (SEQS, LEN, D), 1.0, 6.0, ((0, 4), (1, 8))),
        "positions": draw_positions(jax.random.fold_in(key_of[19], 71), 0),
        "segments": draw_segments(jax.random.fold_in(key_of[19], 71), 0),
        "qkv_weight": normal_values(key_of[4], (D, (QH + 2) * HEAD), D ** -0.5, 0.25, ((1, 4),), jnp.float32),
        "out_weight": normal_values(key_of[5], (QH * HEAD, D), (QH * HEAD) ** -0.5, 0.1875, ((0, 4),), jnp.float32),
        "ff_in_weight": normal_values(key_of[6], (2, D, FF), D ** -0.5, 0.25, ((2, 4),), jnp.float32),
        "ff_out_weight": normal_values(key_of[7], (FF, D), FF ** -0.5, 0.125, ((0, 4),), jnp.float32),
        "norm_gains": jnp.clip(1.0 + 0.1 * jax.random.normal(key_of[8], (GAINS,), jnp.float32), 0.5, 1.5),
        "qkv_moment": draw_qkv_moment(jax.random.fold_in(key_of[19], 71), 0),
        "qkv_square": jnp.clip(jnp.exp(math.log(6898.0) - 1.3865843422731479 * jax.random.uniform(key_of[10], (D, (QH + 2) * HEAD), jnp.float32) ** steps_of(key_of[10], (D, (QH + 2) * HEAD), ((1, 4),), -0.2, 0.2)), 1724.0, 6898.0),
        "out_moment": draw_out_moment(jax.random.fold_in(key_of[19], 71), 0),
        "out_square": jnp.clip(jnp.exp(math.log(6898.0) - 1.3865843422731479 * jax.random.uniform(key_of[12], (QH * HEAD, D), jnp.float32) ** steps_of(key_of[12], (QH * HEAD, D), ((0, 4),), -0.2, 0.2)), 1724.0, 6898.0),
        "ff_in_moment": draw_ff_in_moment(jax.random.fold_in(key_of[19], 71), 0),
        "ff_in_square": jnp.clip(jnp.exp(math.log(6898.0) - 1.3865843422731479 * jax.random.uniform(key_of[14], (2, D, FF), jnp.float32) ** steps_of(key_of[14], (2, D, FF), ((2, 4),), -0.2, 0.2)), 1724.0, 6898.0),
        "ff_out_moment": draw_ff_out_moment(jax.random.fold_in(key_of[19], 71), 0),
        "ff_out_square": jnp.clip(jnp.exp(math.log(6898.0) - 1.3865843422731479 * jax.random.uniform(key_of[16], (FF, D), jnp.float32) ** steps_of(key_of[16], (FF, D), ((0, 4),), -0.2, 0.2)), 1724.0, 6898.0),
        "gains_moment": draw_gains_moment(jax.random.fold_in(key_of[19], 71), 0),
        "gains_square": jnp.clip(jnp.exp(math.log(6898.0) - 1.3865843422731479 * jax.random.uniform(key_of[18], (GAINS,), jnp.float32) ** steps_of(key_of[18], (GAINS,), ((0, 4),), -0.2, 0.2)), 1724.0, 6898.0),
    }


eps_norm = 1e-06
rope_base = 10000.0
beta_first = 0.9
beta_second = 0.95
adam_eps = 1e-08
rate_matrix = 0.05
rate_gain = 0.8
decay_matrix = 0.1
masked_score = -1e+30

@jax.custom_vjp
def low(v):
    return lax.optimization_barrier(v.astype(jnp.bfloat16)).astype(jnp.float32)

@jax.custom_vjp
def low_back(v):
    return v

def low_keep(v):
    return (low(v), None)

def low_pass(kept, grad):
    return (grad,)

def back_keep(v):
    return (v, None)

def back_low(kept, grad):
    return (low(grad),)
low.defvjp(low_keep, low_pass)
low_back.defvjp(back_keep, back_low)

def rms_scale(values, scales):
    return values * lax.rsqrt(lax.optimization_barrier(jnp.mean(values * values, axis=-1, keepdims=True)) + eps_norm) * scales

def rope_tables(positions):
    freqs = 1.0 / rope_base ** (jnp.arange(0, HEAD, 2, dtype=jnp.float32) / HEAD)
    angles = positions.astype(jnp.float32)[..., None] * freqs
    return (jnp.cos(angles), jnp.sin(angles))

def rotate(values, cos_table, sine_table):
    half_width = values.shape[-1] // 2
    first_half = values[..., :half_width]
    second_half = values[..., half_width:]
    return jnp.concatenate([first_half * cos_table - second_half * sine_table, second_half * cos_table + first_half * sine_table], axis=-1)

def split_gains(gain_all):
    return (gain_all[0:D], gain_all[D:2 * D], gain_all[2 * D:3 * D], gain_all[3 * D:4 * D], gain_all[4 * D:4 * D + HEAD], gain_all[4 * D + HEAD:4 * D + 2 * HEAD])

def sequence_forward(inputs, params):
    tokens, positions, segments = inputs
    w_qkv, w_out, w_ffin, w_ffout, gain_all = params
    gain_in, gain_attn, gain_pre, gain_post, gain_query, gain_key = split_gains(gain_all)
    length = tokens.shape[0]
    highest = lax.Precision.HIGHEST
    normed = low(rms_scale(tokens, gain_in))
    project = low_back(jnp.dot(normed, w_qkv, precision=highest))
    cos_table, sine_table = rope_tables(positions)
    queries = project[:, :QH * HEAD].reshape(length, QH, HEAD)
    key_rows = project[:, QH * HEAD:(QH + 1) * HEAD]
    value_rows = project[:, (QH + 1) * HEAD:]
    queries = low(rotate(rms_scale(queries, gain_query), cos_table[:, None], sine_table[:, None]))
    key_rows = low(rotate(rms_scale(key_rows, gain_key), cos_table, sine_table))
    value_rows = low(value_rows)
    key_pad = jnp.concatenate([jnp.zeros((WINDOW, HEAD), key_rows.dtype), key_rows], axis=0)
    value_pad = jnp.concatenate([jnp.zeros((WINDOW, HEAD), value_rows.dtype), value_rows], axis=0)
    segment_pad = jnp.concatenate([jnp.full((WINDOW,), -1, jnp.int32), segments.astype(jnp.int32)])

    def attend(block_index):
        block_start = (block_index * SPAN).astype(jnp.int32)
        query_block = lax.dynamic_slice_in_dim(queries, block_start, SPAN, 0)
        key_block = lax.dynamic_slice_in_dim(key_pad, block_start, WINDOW + SPAN, 0)
        value_block = lax.dynamic_slice_in_dim(value_pad, block_start, WINDOW + SPAN, 0)
        query_segs = lax.dynamic_slice_in_dim(segments.astype(jnp.int32), block_start, SPAN, 0)
        key_segs = lax.dynamic_slice_in_dim(segment_pad, block_start, WINDOW + SPAN, 0)
        distance = jnp.arange(SPAN)[:, None] - (jnp.arange(WINDOW + SPAN)[None, :] - WINDOW)
        allowed = (distance >= 0) & (distance < WINDOW) & (query_segs[:, None] == key_segs[None, :])
        scores = low_back(jnp.einsum('qhd,kd->hqk', query_block, key_block, precision=highest) * HEAD ** (-0.5))
        scores = jnp.where(allowed[None], scores, masked_score)
        attn_probs = jax.nn.softmax(scores, axis=-1)
        attended = jnp.einsum('hqk,kd->qhd', low(attn_probs), value_block, precision=highest)
        return attended.reshape(SPAN, QH * HEAD)
    attended = lax.map(jax.checkpoint(attend), jnp.arange(length // SPAN, dtype=jnp.int32))
    attended = low_back(low(attended.reshape(length, QH * HEAD)))
    branch = low_back(jnp.dot(attended, w_out, precision=highest))
    middle = tokens + rms_scale(branch, gain_attn)
    normed_two = low(rms_scale(middle, gain_pre))
    gate_proj = low_back(jnp.dot(normed_two, w_ffin[0], precision=highest))
    upward = low_back(jnp.dot(normed_two, w_ffin[1], precision=highest))
    hidden = low(jax.nn.gelu(gate_proj, approximate=True) * upward)
    branch_two = low_back(jnp.dot(hidden, w_ffout, precision=highest))
    return middle + rms_scale(branch_two, gain_post)

def forward(tokens, w_qkv, w_out, w_ffin, w_ffout, gain_all, positions, segments):
    lowered = (low(w_qkv), low(w_out), low(w_ffin), low(w_ffout), low(gain_all))
    step_fn = jax.checkpoint(partial(sequence_forward, params=lowered))
    return lax.map(step_fn, (tokens, positions, segments))

def adam_step(weight, gradient, moment, square, step_rate, decay_rate):
    moment_new = beta_first * moment + (1.0 - beta_first) * gradient
    square_new = beta_second * square + (1.0 - beta_second) * gradient * gradient
    moment_hat = moment_new / (1.0 - beta_first ** STEP)
    square_hat = square_new / (1.0 - beta_second ** STEP)
    weight_new = weight - step_rate * (moment_hat / (jnp.sqrt(square_hat) + adam_eps) + decay_rate * weight)
    return (weight_new, moment_new, square_new)

def reference(block_input, out_grad, positions, segments, qkv_weight, out_weight, ff_in_weight, ff_out_weight, norm_gains, qkv_moment, qkv_square, out_moment, out_square, ff_in_moment, ff_in_square, ff_out_moment, ff_out_square, gains_moment, gains_square):
    tokens = block_input.astype(jnp.float32)
    outputs, pullback = jax.vjp(partial(forward, positions=positions, segments=segments), tokens, qkv_weight, out_weight, ff_in_weight, ff_out_weight, norm_gains)
    grads = pullback(out_grad.astype(jnp.float32))
    qkv_new = adam_step(qkv_weight, grads[1], qkv_moment, qkv_square, rate_matrix, decay_matrix)
    out_new = adam_step(out_weight, grads[2], out_moment, out_square, rate_matrix, decay_matrix)
    ffin_new = adam_step(ff_in_weight, grads[3], ff_in_moment, ff_in_square, rate_matrix, decay_matrix)
    ffout_new = adam_step(ff_out_weight, grads[4], ff_out_moment, ff_out_square, rate_matrix, decay_matrix)
    gains_new = adam_step(norm_gains, grads[5], gains_moment, gains_square, rate_gain, 0.0)
    return (outputs.astype(jnp.bfloat16), grads[0].astype(jnp.bfloat16), qkv_new[0], qkv_new[1], qkv_new[2], out_new[0], out_new[1], out_new[2], ffin_new[0], ffin_new[1], ffin_new[2], ffout_new[0], ffout_new[1], ffout_new[2], gains_new[0], gains_new[1], gains_new[2])
```

```python
from functools import partial

import jax
import jax.numpy as jnp
from jax import lax
from jax.sharding import PartitionSpec as P

D = 640
QH = 4
HEAD = 256
WINDOW = 512
STEP = 10


eps_norm = 1e-06
rope_base = 10000.0
beta_first = 0.9
beta_second = 0.95
adam_eps = 1e-08
rate_matrix = 0.05
rate_gain = 0.8
decay_matrix = 0.1
masked_score = -1e30


def from_behind(block, axis, distance):
    devices = range(lax.axis_size(axis))
    route = [(i - distance, i) for i in devices if i - distance in devices]
    return lax.ppermute(block, axis, route)


def swap_bit(block, axis, bit):
    return lax.ppermute(block, axis, [(i, i ^ (1 << bit)) for i in range(lax.axis_size(axis))])


def my_bit(axis, bit):
    return (lax.axis_index(axis) >> bit) & 1


def halve(block, axis, bit, at):
    mine = my_bit(axis, bit)
    sent = lax.dynamic_index_in_dim(block, 1 - mine, at, keepdims=False)
    kept = lax.dynamic_index_in_dim(block, mine, at, keepdims=False)
    came = swap_bit(sent, axis, bit)
    return (kept.astype(jnp.float32) + came.astype(jnp.float32)).astype(jnp.bfloat16)


def bits_of(axis):
    return lax.axis_size(axis).bit_length() - 1


def reduce_steps(block):
    for bit in range(bits_of("shard")):
        block = halve(block.reshape((-1, 2) + block.shape[1:]), "shard", bit, 1)
        block = yield block
    block = block[0]
    for bit in range(bits_of("seq")):
        block = halve(block.reshape((2, -1) + block.shape[1:]), "seq", bit, 0)
        block = yield block
    for bit in reversed(range(bits_of("seq"))):
        came = swap_bit(block, "seq", bit)
        low = my_bit("seq", bit) == 0
        block = jnp.concatenate([jnp.where(low, block, came), jnp.where(low, came, block)], axis=0)
        block = yield block


def advance(steps, block):
    try:
        return steps.send(block)
    except StopIteration:
        return block


def finish(steps, block):
    while True:
        try:
            block = steps.send(block)
        except StopIteration:
            return block


def together(*values):
    return lax.optimization_barrier(values)


def rms_scale(values, scales):
    return values * lax.rsqrt(jnp.mean(values * values, axis=-1, keepdims=True) + eps_norm) * scales


def rope_tables(positions):
    freqs = 1.0 / rope_base ** (jnp.arange(0, HEAD, 2, dtype=jnp.float32) / HEAD)
    angles = positions.astype(jnp.float32)[..., None] * freqs
    return (jnp.cos(angles), jnp.sin(angles))


def rotate(values, cos_table, sine_table):
    half_width = values.shape[-1] // 2
    first_half = values[..., :half_width]
    second_half = values[..., half_width:]
    return jnp.concatenate(
        [
            first_half * cos_table - second_half * sine_table,
            second_half * cos_table + first_half * sine_table,
        ],
        axis=-1,
    )


def split_gains(gain_all):
    return (
        gain_all[0:D],
        gain_all[D : 2 * D],
        gain_all[2 * D : 3 * D],
        gain_all[3 * D : 4 * D],
        gain_all[4 * D : 4 * D + HEAD],
        gain_all[4 * D + HEAD : 4 * D + 2 * HEAD],
    )


def head_post(project, gain_query, gain_key, cos_table, sine_table):
    queries = project[..., : QH * HEAD].reshape(project.shape[:-1] + (QH, HEAD))
    key_rows = project[..., QH * HEAD : (QH + 1) * HEAD]
    value_rows = project[..., (QH + 1) * HEAD :]
    queries = rotate(
        rms_scale(queries, gain_query), cos_table[..., None, :], sine_table[..., None, :]
    )
    key_rows = rotate(rms_scale(key_rows, gain_key), cos_table, sine_table)
    return (queries, key_rows, value_rows)


def score_block(queries, key_rows, allowed):
    scores = jnp.einsum(
        "sqhd,skd->shqk", queries, key_rows, preferred_element_type=jnp.float32
    ) * HEAD ** (-0.5)
    return jnp.where(allowed[:, None], scores, masked_score)


def adam_step(weight, gradient, moment, square, step_rate, decay_rate):
    moment_new = beta_first * moment + (1.0 - beta_first) * gradient
    square_new = beta_second * square + (1.0 - beta_second) * gradient * gradient
    moment_hat = moment_new / (1.0 - beta_first**STEP)
    square_hat = square_new / (1.0 - beta_second**STEP)
    weight_new = weight - step_rate * (
        moment_hat / (jnp.sqrt(square_hat) + adam_eps) + decay_rate * weight
    )
    return (weight_new, moment_new, square_new)


def on_device(
    block_input,
    out_grad,
    positions,
    segments,
    qkv_weight,
    out_weight,
    ff_in_weight,
    ff_out_weight,
    norm_gains,
    qkv_moment,
    qkv_square,
    out_moment,
    out_square,
    ff_in_moment,
    ff_in_square,
    ff_out_moment,
    ff_out_square,
    gains_moment,
    gains_square,
):
    seqs_here, span_rows, model_width = block_input.shape
    row_count = seqs_here * span_rows
    w_qkv, w_out, w_ffin, w_ffout, gains_low = (
        lax.all_gather(qkv_weight.astype(jnp.bfloat16), "shard", axis=1, tiled=True),
        lax.all_gather(out_weight.astype(jnp.bfloat16), "shard", axis=0, tiled=True),
        lax.all_gather(ff_in_weight.astype(jnp.bfloat16), "shard", axis=2, tiled=True),
        lax.all_gather(ff_out_weight.astype(jnp.bfloat16), "shard", axis=0, tiled=True),
        lax.all_gather(norm_gains.astype(jnp.bfloat16), "shard", axis=0, tiled=True),
    )
    gain_in, gain_attn, gain_pre, gain_post, gain_query, gain_key = split_gains(
        gains_low.astype(jnp.float32)
    )
    tokens = block_input.astype(jnp.float32).reshape(row_count, model_width)
    normed = rms_scale(tokens, gain_in).astype(jnp.bfloat16)
    project = jnp.dot(normed, w_qkv, preferred_element_type=jnp.float32).reshape(
        seqs_here, span_rows, -1
    )
    cos_table, sine_table = rope_tables(positions)
    query_full, key_full, value_full = head_post(
        project, gain_query, gain_key, cos_table, sine_table
    )
    queries = query_full.astype(jnp.bfloat16)
    keys_own = key_full.astype(jnp.bfloat16)
    values_own = value_full.astype(jnp.bfloat16)
    key_prev, value_prev, segment_prev = from_behind((keys_own, values_own, segments), "seq", 1)
    is_first = lax.axis_index("seq") == 0
    distance = jnp.arange(span_rows)[:, None] - (jnp.arange(WINDOW + span_rows)[None, :] - WINDOW)
    in_window = (distance >= 0) & (distance < WINDOW)
    from_prev = (jnp.arange(WINDOW + span_rows) >= WINDOW) | jnp.logical_not(is_first)
    key_segments = jnp.concatenate([segment_prev, segments], axis=1)
    same_doc = segments[:, :, None] == key_segments[:, None, :]
    allowed = in_window[None] & from_prev[None, None, :] & same_doc
    all_keys = jnp.concatenate([key_prev, keys_own], axis=1)
    all_values = jnp.concatenate([value_prev, values_own], axis=1)
    scores = score_block(queries, all_keys, allowed)
    row_top = jnp.max(scores, axis=-1, keepdims=True)
    exp_terms = jnp.exp(scores - row_top)
    row_total = jnp.sum(exp_terms, axis=-1, keepdims=True)
    attn_probs = exp_terms / row_total
    log_total = row_top + jnp.log(row_total)
    attended = jnp.einsum(
        "shqk,skd->sqhd",
        attn_probs.astype(jnp.bfloat16),
        all_values,
        preferred_element_type=jnp.float32,
    )
    attended_low = attended.reshape(row_count, QH * HEAD).astype(jnp.bfloat16)
    branch = jnp.dot(attended_low, w_out, preferred_element_type=jnp.float32)
    middle = tokens + rms_scale(branch, gain_attn)
    normed_two = rms_scale(middle, gain_pre).astype(jnp.bfloat16)
    gate_proj = jnp.dot(normed_two, w_ffin[0], preferred_element_type=jnp.float32)
    upward = jnp.dot(normed_two, w_ffin[1], preferred_element_type=jnp.float32)
    hidden = (jax.nn.gelu(gate_proj, approximate=True) * upward).astype(jnp.bfloat16)
    branch_two = jnp.dot(hidden, w_ffout, preferred_element_type=jnp.float32)
    mixed = (
        (middle + rms_scale(branch_two, gain_post))
        .astype(jnp.bfloat16)
        .reshape(seqs_here, span_rows, model_width)
    )
    cotangent = out_grad.astype(jnp.float32).reshape(row_count, model_width)
    post_back = jax.vjp(rms_scale, branch_two, gain_post)[1]
    grad_branch_two, grad_gain_post = post_back(cotangent)
    grad_ffn_low = grad_branch_two.astype(jnp.bfloat16)
    grad_hidden = jnp.einsum("nd,fd->nf", grad_ffn_low, w_ffout, preferred_element_type=jnp.float32)
    gelu_back = jax.vjp(
        lambda gate_in, up_in: jax.nn.gelu(gate_in, approximate=True) * up_in, gate_proj, upward
    )[1]
    grad_gate, grad_up = gelu_back(grad_hidden)
    grad_gate_low = grad_gate.astype(jnp.bfloat16)
    grad_up_low = grad_up.astype(jnp.bfloat16)
    shards = lax.axis_size("shard")
    low_dot = partial(jnp.einsum, preferred_element_type=jnp.float32)
    ffn_parts = jnp.concatenate(
        [
            part.astype(jnp.bfloat16).reshape(model_width, shards, -1).swapaxes(0, 1)
            for part in (
                low_dot("nd,nf->df", normed_two, grad_gate_low),
                low_dot("nd,nf->df", normed_two, grad_up_low),
                low_dot("nd,nf->df", grad_ffn_low, hidden),
            )
        ],
        axis=1,
    )
    grad_gate_low, grad_up_low, ffn_parts = together(grad_gate_low, grad_up_low, ffn_parts)
    ffn_steps = reduce_steps(ffn_parts)
    ffn_sum = next(ffn_steps)
    grad_normed_two = jnp.einsum(
        "nf,df->nd", grad_gate_low, w_ffin[0], preferred_element_type=jnp.float32
    ) + jnp.einsum("nf,df->nd", grad_up_low, w_ffin[1], preferred_element_type=jnp.float32)
    pre_back = jax.vjp(rms_scale, middle, gain_pre)[1]
    grad_middle_ffn, grad_gain_pre = pre_back(grad_normed_two)
    grad_middle = cotangent + grad_middle_ffn
    attn_back = jax.vjp(rms_scale, branch, gain_attn)[1]
    grad_branch, grad_gain_attn = attn_back(grad_middle)
    grad_attn_low = grad_branch.astype(jnp.bfloat16)
    grad_attended = jnp.einsum(
        "nd,kd->nk", grad_attn_low, w_out, preferred_element_type=jnp.float32
    )
    grad_attended = grad_attended.astype(jnp.bfloat16).reshape(seqs_here, span_rows, QH, HEAD)
    grad_attended, ffn_sum = together(grad_attended, ffn_sum)
    ffn_sum = advance(ffn_steps, ffn_sum)
    scores_back = score_block(queries, all_keys, allowed)
    probs_back = jnp.exp(scores_back - log_total)
    grad_values = jnp.einsum(
        "shqk,sqhd->skd",
        probs_back.astype(jnp.bfloat16),
        grad_attended,
        preferred_element_type=jnp.float32,
    )
    grad_probs = jnp.einsum(
        "sqhd,skd->shqk", grad_attended, all_values, preferred_element_type=jnp.float32
    )
    inner_sum = jnp.sum(probs_back * grad_probs, axis=-1, keepdims=True)
    grad_scores = (probs_back * (grad_probs - inner_sum)).astype(jnp.bfloat16)
    grad_scores, ffn_sum = together(grad_scores, ffn_sum)
    ffn_sum = advance(ffn_steps, ffn_sum)
    grad_queries = jnp.einsum(
        "shqk,skd->sqhd", grad_scores, all_keys, preferred_element_type=jnp.float32
    ) * HEAD ** (-0.5)
    grad_keys = jnp.einsum(
        "shqk,sqhd->skd", grad_scores, queries, preferred_element_type=jnp.float32
    ) * HEAD ** (-0.5)
    grad_key_next, grad_value_next = (
        from_behind(grad_keys[:, :WINDOW].astype(jnp.bfloat16), "seq", -1).astype(jnp.float32),
        from_behind(grad_values[:, :WINDOW].astype(jnp.bfloat16), "seq", -1).astype(jnp.float32),
    )
    grad_key_own = grad_keys[:, WINDOW:] + grad_key_next
    grad_value_own = grad_values[:, WINDOW:] + grad_value_next
    head_back = jax.vjp(
        partial(head_post, cos_table=cos_table, sine_table=sine_table),
        project,
        gain_query,
        gain_key,
    )[1]
    grad_project, grad_gain_query, grad_gain_key = head_back(
        (grad_queries, grad_key_own, grad_value_own)
    )
    grad_project_low = grad_project.reshape(row_count, -1).astype(jnp.bfloat16)
    grad_project_low, ffn_sum = together(grad_project_low, ffn_sum)
    ffn_sum = advance(ffn_steps, ffn_sum)
    attn_parts = jnp.concatenate(
        [
            part.astype(jnp.bfloat16).reshape(model_width, shards, -1).swapaxes(0, 1)
            for part in (
                low_dot("nd,nk->dk", normed, grad_project_low),
                low_dot("nd,nk->dk", grad_attn_low, attended_low),
            )
        ],
        axis=2,
    )
    grad_project_low, attn_parts = together(grad_project_low, attn_parts)
    attn_steps = reduce_steps(attn_parts)
    attn_total = finish(attn_steps, next(attn_steps))
    ffn_total = finish(ffn_steps, ffn_sum)
    grad_normed = jnp.einsum(
        "nk,dk->nd", grad_project_low, w_qkv, preferred_element_type=jnp.float32
    )
    in_back = jax.vjp(rms_scale, tokens, gain_in)[1]
    grad_tokens, grad_gain_in = in_back(grad_normed)
    input_grad = (
        (grad_middle + grad_tokens).astype(jnp.bfloat16).reshape(seqs_here, span_rows, model_width)
    )
    grad_gains = jnp.concatenate(
        [
            grad_gain_in,
            grad_gain_attn,
            grad_gain_pre,
            grad_gain_post,
            grad_gain_query,
            grad_gain_key,
        ]
    )
    masters = (qkv_weight, out_weight, ff_in_weight, ff_out_weight, norm_gains)
    moments = (qkv_moment, out_moment, ff_in_moment, ff_out_moment, gains_moment)
    squares = (qkv_square, out_square, ff_in_square, ff_out_square, gains_square)
    step_rates = (rate_matrix, rate_matrix, rate_matrix, rate_matrix, rate_gain)
    decays = (decay_matrix, decay_matrix, decay_matrix, decay_matrix, 0.0)
    gains_here = norm_gains.shape[0]
    gains_total = lax.dynamic_slice_in_dim(
        lax.psum(grad_gains, ("shard", "seq")), lax.axis_index("shard") * gains_here, gains_here
    )
    qkv_here = qkv_weight.shape[1]
    attn_total, ffn_total = together(attn_total, ffn_total)
    down_total, out_total = together(ffn_total[2 * model_width :].T, attn_total[:, qkv_here:].T)
    totals = (
        attn_total[:, :qkv_here].astype(jnp.float32),
        out_total.astype(jnp.float32),
        ffn_total[: 2 * model_width].reshape(ff_in_weight.shape).astype(jnp.float32),
        down_total.astype(jnp.float32),
        gains_total,
    )
    results = [
        adam_step(
            masters[weight_index],
            totals[weight_index],
            moments[weight_index],
            squares[weight_index],
            step_rates[weight_index],
            decays[weight_index],
        )
        for weight_index in range(5)
    ]
    return (
        mixed,
        input_grad,
        results[0][0],
        results[0][1],
        results[0][2],
        results[1][0],
        results[1][1],
        results[1][2],
        results[2][0],
        results[2][1],
        results[2][2],
        results[3][0],
        results[3][1],
        results[3][2],
        results[4][0],
        results[4][1],
        results[4][2],
    )


def solution(mesh):
    return jax.shard_map(
        on_device,
        mesh=mesh,
        in_specs=(
            P("shard", "seq", None),
            P("shard", "seq", None),
            P("shard", "seq"),
            P("shard", "seq"),
            P(None, "shard"),
            P("shard", None),
            P(None, None, "shard"),
            P("shard", None),
            P("shard"),
            P(None, "shard"),
            P(None, "shard"),
            P("shard", None),
            P("shard", None),
            P(None, None, "shard"),
            P(None, None, "shard"),
            P("shard", None),
            P("shard", None),
            P("shard"),
            P("shard"),
        ),
        out_specs=(
            P("shard", "seq", None),
            P("shard", "seq", None),
            P(None, "shard"),
            P(None, "shard"),
            P(None, "shard"),
            P("shard", None),
            P("shard", None),
            P("shard", None),
            P(None, None, "shard"),
            P(None, None, "shard"),
            P(None, None, "shard"),
            P("shard", None),
            P("shard", None),
            P("shard", None),
            P("shard"),
            P("shard"),
            P("shard"),
        ),
        check_vma=False,
    )
```

```python
from functools import partial

import jax
import jax.numpy as jnp
from jax import lax
from jax.experimental import pallas as pl
from jax.experimental.pallas import tpu as pltpu
from jax.sharding import PartitionSpec as P

D = 640
QH = 4
HEAD = 256
WINDOW = 512
STEP = 10


eps_norm = 1e-06
rope_base = 10000.0
beta_first = 0.9
beta_second = 0.95
adam_eps = 1e-08
rate_matrix = 0.05
rate_gain = 0.8
decay_matrix = 0.1
masked_score = -1e30


def from_behind(block, axis, distance):
    devices = range(lax.axis_size(axis))
    route = [(i - distance, i) for i in devices if i - distance in devices]
    return lax.ppermute(block, axis, route)


def swap_bit(block, axis, bit):
    return lax.ppermute(block, axis, [(i, i ^ (1 << bit)) for i in range(lax.axis_size(axis))])


def my_bit(axis, bit):
    return (lax.axis_index(axis) >> bit) & 1


def halve(block, axis, bit, at):
    mine = my_bit(axis, bit)
    sent = lax.dynamic_index_in_dim(block, 1 - mine, at, keepdims=False)
    kept = lax.dynamic_index_in_dim(block, mine, at, keepdims=False)
    came = swap_bit(sent, axis, bit)
    return (kept.astype(jnp.float32) + came.astype(jnp.float32)).astype(jnp.bfloat16)


def bits_of(axis):
    return lax.axis_size(axis).bit_length() - 1


def reduce_steps(block):
    for bit in range(bits_of("shard")):
        block = halve(block.reshape((-1, 2) + block.shape[1:]), "shard", bit, 1)
        block = yield block
    block = block[0]
    for bit in range(bits_of("seq")):
        block = halve(block.reshape((2, -1) + block.shape[1:]), "seq", bit, 0)
        block = yield block
    for bit in reversed(range(bits_of("seq"))):
        came = swap_bit(block, "seq", bit)
        low = my_bit("seq", bit) == 0
        block = jnp.concatenate([jnp.where(low, block, came), jnp.where(low, came, block)], axis=0)
        block = yield block


def advance(steps, block):
    try:
        return steps.send(block)
    except StopIteration:
        return block


def finish(steps, block):
    while True:
        try:
            block = steps.send(block)
        except StopIteration:
            return block


def together(*values):
    return lax.optimization_barrier(values)


def rms_scale(values, scales):
    return values * lax.rsqrt(jnp.mean(values * values, axis=-1, keepdims=True) + eps_norm) * scales


def rope_tables(positions):
    freqs = 1.0 / rope_base ** (jnp.arange(0, HEAD, 2, dtype=jnp.float32) / HEAD)
    angles = positions.astype(jnp.float32)[..., None] * freqs
    return (jnp.cos(angles), jnp.sin(angles))


def rotate(values, cos_table, sine_table):
    half_width = values.shape[-1] // 2
    first_half = values[..., :half_width]
    second_half = values[..., half_width:]
    return jnp.concatenate(
        [
            first_half * cos_table - second_half * sine_table,
            second_half * cos_table + first_half * sine_table,
        ],
        axis=-1,
    )


def split_gains(gain_all):
    return (
        gain_all[0:D],
        gain_all[D : 2 * D],
        gain_all[2 * D : 3 * D],
        gain_all[3 * D : 4 * D],
        gain_all[4 * D : 4 * D + HEAD],
        gain_all[4 * D + HEAD : 4 * D + 2 * HEAD],
    )


def head_post(project, gain_query, gain_key, cos_table, sine_table):
    queries = project[..., : QH * HEAD].reshape(project.shape[:-1] + (QH, HEAD))
    key_rows = project[..., QH * HEAD : (QH + 1) * HEAD]
    value_rows = project[..., (QH + 1) * HEAD :]
    queries = rotate(
        rms_scale(queries, gain_query), cos_table[..., None, :], sine_table[..., None, :]
    )
    key_rows = rotate(rms_scale(key_rows, gain_key), cos_table, sine_table)
    return (queries, key_rows, value_rows)


f32 = jnp.float32
bf16 = jnp.bfloat16
row_block = 256
vmem_most = 56 * 1024 * 1024


def dot_nn(a, b):
    return lax.dot_general(a, b, (((1,), (0,)), ((), ())), preferred_element_type=f32)


def dot_nt(a, b):
    return lax.dot_general(a, b, (((1,), (1,)), ((), ())), preferred_element_type=f32)


def inverse_rms(v):
    return lax.rsqrt(jnp.mean(v * v, axis=-1, keepdims=True) + eps_norm)


def rms_back(v, r, gain, dy):
    gdy = gain * dy
    return r * gdy - v * (r * r * r) * jnp.mean(gdy * v, axis=-1, keepdims=True)


def middle_kernel(
    blocks, shards,
    x_ref, o_ref, e_ref, w_out_ref, w_in_ref, w_down_ref, gains_ref,
    mixed_ref, dx2_ref, do_ref, ffn_ref, out_ref, dgains_ref,
    act, slope, h2_all, dm_all, db_all, o_all, hid_all, dg_all, du_all,
):
    step = pl.program_id(0)
    ff = w_in_ref.shape[3]
    model = x_ref.shape[1]
    heads = out_ref.shape[2]

    @pl.when(step < blocks)
    def _():
        rows = pl.ds(pl.multiple_of(step * row_block, row_block), row_block)
        gain_attn, gain_pre, gain_post = gains_ref[0:1], gains_ref[1:2], gains_ref[2:3]
        x = x_ref[...].astype(f32)
        e = e_ref[...].astype(f32)
        o = o_ref[...]
        branch = dot_nn(o, w_out_ref[...])
        r_branch = inverse_rms(branch)
        x2 = x + branch * r_branch * gain_attn
        r_x2 = inverse_rms(x2)
        h2 = (x2 * r_x2 * gain_pre).astype(bf16)
        m = jnp.zeros((row_block, model), f32)
        for s in range(shards):
            cols = slice(s * ff, (s + 1) * ff)
            gate = dot_nn(h2, w_in_ref[s, 0])
            up = dot_nn(h2, w_in_ref[s, 1])
            c = (2.0 / jnp.pi) ** 0.5
            sq = gate * gate
            t = jnp.tanh(c * gate * (1.0 + 0.044715 * sq))
            half = 0.5 * (1.0 + t)
            gelu = gate * half
            act[:, cols] = gelu
            slope[:, cols] = up * (
                half + 0.5 * gate * (1.0 - t * t) * (c * (1.0 + 3 * 0.044715 * sq))
            )
            hidden = (gelu * up).astype(bf16)
            hid_all[s, rows] = hidden
            m += dot_nn(hidden, w_down_ref[s])
        r_m = inverse_rms(m)
        mixed_ref[...] = (x2 + m * r_m * gain_post).astype(bf16)
        dm = rms_back(m, r_m, gain_post, e).astype(bf16)
        dh2 = jnp.zeros((row_block, model), f32)
        for s in range(shards):
            cols = slice(s * ff, (s + 1) * ff)
            dh = dot_nt(dm, w_down_ref[s])
            dgate = (dh * slope[:, cols]).astype(bf16)
            dup = (dh * act[:, cols]).astype(bf16)
            dg_all[s, rows] = dgate
            du_all[s, rows] = dup
            dh2 += dot_nt(dgate, w_in_ref[s, 0]) + dot_nt(dup, w_in_ref[s, 1])
        dx2 = e + rms_back(x2, r_x2, gain_pre, dh2)
        dx2_ref[...] = dx2
        db = rms_back(branch, r_branch, gain_attn, dx2).astype(bf16)
        do_ref[...] = dot_nt(db, w_out_ref[...]).astype(bf16)
        h2_all[rows] = h2
        dm_all[rows] = dm
        db_all[rows] = db
        for s in range(shards):
            o_all[s, rows] = o[:, s * heads : (s + 1) * heads]

        @pl.when(step == 0)
        def _():
            dgains_ref[...] = jnp.zeros_like(dgains_ref)

        dgains_ref[0:1] += jnp.sum(dx2 * branch * r_branch, axis=0, keepdims=True)
        dgains_ref[1:2] += jnp.sum(dh2 * x2 * r_x2, axis=0, keepdims=True)
        dgains_ref[2:3] += jnp.sum(e * m * r_m, axis=0, keepdims=True)

    @pl.when(step >= blocks)
    def _():
        s = step - blocks
        h2_t = h2_all[...].T
        ffn_ref[0, 0:model] = dot_nn(h2_t, dg_all[s]).astype(bf16)
        ffn_ref[0, model : 2 * model] = dot_nn(h2_t, du_all[s]).astype(bf16)
        ffn_ref[0, 2 * model : 3 * model] = dot_nn(dm_all[...].T, hid_all[s]).astype(bf16)
        out_ref[0] = dot_nn(db_all[...].T, o_all[s]).astype(bf16)


def middle(x, attended, out_grad, w_out, w_in, w_down, gains):
    rows, model = x.shape
    inner = attended.shape[1]
    shards, _, _, ff = w_in.shape
    blocks = rows // row_block
    heads = inner // shards

    def row_spec(width):
        return pl.BlockSpec((row_block, width), lambda i: (jnp.minimum(i, blocks - 1), 0))

    def whole(shape):
        return pl.BlockSpec(shape, lambda i: (0,) * len(shape), pipeline_mode=pl.Buffered(1))

    def shard_spec(shape):
        return pl.BlockSpec((1,) + shape, lambda i: (jnp.maximum(i - blocks, 0), 0, 0))

    return pl.pallas_call(
        partial(middle_kernel, blocks, shards),
        grid=(blocks + shards,),
        in_specs=[
            row_spec(model), row_spec(inner), row_spec(model),
            whole(w_out.shape), whole(w_in.shape), whole(w_down.shape), whole(gains.shape),
        ],
        out_specs=[
            row_spec(model), row_spec(model), row_spec(inner),
            shard_spec((3 * model, ff)), shard_spec((model, heads)),
            pl.BlockSpec((8, model), lambda i: (0, 0)),
        ],
        out_shape=[
            jax.ShapeDtypeStruct((rows, model), bf16),
            jax.ShapeDtypeStruct((rows, model), f32),
            jax.ShapeDtypeStruct((rows, inner), bf16),
            jax.ShapeDtypeStruct((shards, 3 * model, ff), bf16),
            jax.ShapeDtypeStruct((shards, model, heads), bf16),
            jax.ShapeDtypeStruct((8, model), f32),
        ],
        scratch_shapes=[
            pltpu.VMEM((row_block, shards * ff), f32),
            pltpu.VMEM((row_block, shards * ff), f32),
            pltpu.VMEM((rows, model), bf16),
            pltpu.VMEM((rows, model), bf16),
            pltpu.VMEM((rows, model), bf16),
            pltpu.VMEM((shards, rows, heads), bf16),
            pltpu.VMEM((shards, rows, ff), bf16),
            pltpu.VMEM((shards, rows, ff), bf16),
            pltpu.VMEM((shards, rows, ff), bf16),
        ],
        compiler_params=pltpu.CompilerParams(vmem_limit_bytes=vmem_most),
        cost_estimate=pl.CostEstimate(
            flops=2 * rows * model * 3 * (3 * shards * ff + inner),
            bytes_accessed=30 << 20, transcendentals=rows * shards * ff,
        ),
        name="middle",
    )(x, attended, out_grad, w_out, w_in, w_down, gains)


def turn_kernel(ffn_ref, attn_ref, down_ref, out_ref):
    down_ref[...] = ffn_ref[...].astype(f32).T
    out_ref[...] = attn_ref[...].astype(f32).T


def turn(ffn_part, attn_part):
    return pl.pallas_call(
        turn_kernel,
        out_shape=[
            jax.ShapeDtypeStruct(part.shape[::-1], f32) for part in (ffn_part, attn_part)
        ],
        compiler_params=pltpu.CompilerParams(vmem_limit_bytes=24 * 1024 * 1024),
        name="turn",
    )(ffn_part, attn_part)


def score_block(queries, key_rows, allowed):
    scores = jnp.einsum(
        "sqhd,skd->shqk", queries, key_rows, preferred_element_type=jnp.float32
    ) * HEAD ** (-0.5)
    return jnp.where(allowed[:, None], scores, masked_score)


def adam_step(weight, gradient, moment, square, step_rate, decay_rate):
    moment_new = beta_first * moment + (1.0 - beta_first) * gradient
    square_new = beta_second * square + (1.0 - beta_second) * gradient * gradient
    moment_hat = moment_new / (1.0 - beta_first**STEP)
    square_hat = square_new / (1.0 - beta_second**STEP)
    weight_new = weight - step_rate * (
        moment_hat / (jnp.sqrt(square_hat) + adam_eps) + decay_rate * weight
    )
    return (weight_new, moment_new, square_new)


def on_device(
    block_input,
    out_grad,
    positions,
    segments,
    qkv_weight,
    out_weight,
    ff_in_weight,
    ff_out_weight,
    norm_gains,
    qkv_moment,
    qkv_square,
    out_moment,
    out_square,
    ff_in_moment,
    ff_in_square,
    ff_out_moment,
    ff_out_square,
    gains_moment,
    gains_square,
):
    seqs_here, span_rows, model_width = block_input.shape
    row_count = seqs_here * span_rows
    w_qkv, w_out, w_ffin, w_ffout, gains_low = (
        lax.all_gather(qkv_weight.astype(jnp.bfloat16), "shard", axis=1, tiled=True),
        lax.all_gather(out_weight.astype(jnp.bfloat16), "shard", axis=0, tiled=True),
        lax.all_gather(ff_in_weight.astype(jnp.bfloat16), "shard", axis=0),
        lax.all_gather(ff_out_weight.astype(jnp.bfloat16), "shard", axis=0),
        lax.all_gather(norm_gains.astype(jnp.bfloat16), "shard", axis=0, tiled=True),
    )
    gain_in, gain_attn, gain_pre, gain_post, gain_query, gain_key = split_gains(
        gains_low.astype(jnp.float32)
    )
    tokens = block_input.astype(jnp.float32).reshape(row_count, model_width)
    normed = rms_scale(tokens, gain_in).astype(jnp.bfloat16)
    project = jnp.dot(normed, w_qkv, preferred_element_type=jnp.float32).reshape(
        seqs_here, span_rows, -1
    )
    cos_table, sine_table = rope_tables(positions)
    query_full, key_full, value_full = head_post(
        project, gain_query, gain_key, cos_table, sine_table
    )
    queries = query_full.astype(jnp.bfloat16)
    keys_own = key_full.astype(jnp.bfloat16)
    values_own = value_full.astype(jnp.bfloat16)
    key_prev, value_prev, segment_prev = from_behind((keys_own, values_own, segments), "seq", 1)
    is_first = lax.axis_index("seq") == 0
    distance = jnp.arange(span_rows)[:, None] - (jnp.arange(WINDOW + span_rows)[None, :] - WINDOW)
    in_window = (distance >= 0) & (distance < WINDOW)
    from_prev = (jnp.arange(WINDOW + span_rows) >= WINDOW) | jnp.logical_not(is_first)
    key_segments = jnp.concatenate([segment_prev, segments], axis=1)
    same_doc = segments[:, :, None] == key_segments[:, None, :]
    allowed = in_window[None] & from_prev[None, None, :] & same_doc
    all_keys = jnp.concatenate([key_prev, keys_own], axis=1)
    all_values = jnp.concatenate([value_prev, values_own], axis=1)
    scores = score_block(queries, all_keys, allowed)
    row_top = jnp.max(scores, axis=-1, keepdims=True)
    exp_terms = jnp.exp(scores - row_top)
    row_total = jnp.sum(exp_terms, axis=-1, keepdims=True)
    attn_probs = exp_terms / row_total
    log_total = row_top + jnp.log(row_total)
    attended = jnp.einsum(
        "shqk,skd->sqhd",
        attn_probs.astype(jnp.bfloat16),
        all_values,
        preferred_element_type=jnp.float32,
    )
    attended_low = attended.reshape(row_count, QH * HEAD).astype(jnp.bfloat16)
    shards = lax.axis_size("shard")
    low_dot = partial(jnp.einsum, preferred_element_type=jnp.float32)
    mixed, grad_middle, grad_attended, ffn_parts, out_parts, grad_three = middle(
        block_input.reshape(row_count, model_width),
        attended_low,
        out_grad.reshape(row_count, model_width),
        w_out,
        w_ffin,
        w_ffout,
        jnp.stack([gain_attn, gain_pre, gain_post]),
    )
    mixed = mixed.reshape(block_input.shape)
    grad_gain_attn, grad_gain_pre, grad_gain_post = grad_three[0], grad_three[1], grad_three[2]
    grad_attended = grad_attended.reshape(seqs_here, span_rows, QH, HEAD)
    ffn_steps = reduce_steps(ffn_parts)
    ffn_sum = next(ffn_steps)
    scores_back = score_block(queries, all_keys, allowed)
    scores_back, ffn_sum = together(scores_back, ffn_sum)
    ffn_sum = advance(ffn_steps, ffn_sum)
    probs_back = jnp.exp(scores_back - log_total)
    grad_values = jnp.einsum(
        "shqk,sqhd->skd",
        probs_back.astype(jnp.bfloat16),
        grad_attended,
        preferred_element_type=jnp.float32,
    )
    grad_probs = jnp.einsum(
        "sqhd,skd->shqk", grad_attended, all_values, preferred_element_type=jnp.float32
    )
    inner_sum = jnp.sum(probs_back * grad_probs, axis=-1, keepdims=True)
    grad_scores = (probs_back * (grad_probs - inner_sum)).astype(jnp.bfloat16)
    grad_scores, ffn_sum = together(grad_scores, ffn_sum)
    ffn_sum = advance(ffn_steps, ffn_sum)
    grad_queries = jnp.einsum(
        "shqk,skd->sqhd", grad_scores, all_keys, preferred_element_type=jnp.float32
    ) * HEAD ** (-0.5)
    grad_keys = jnp.einsum(
        "shqk,sqhd->skd", grad_scores, queries, preferred_element_type=jnp.float32
    ) * HEAD ** (-0.5)
    grad_key_next, grad_value_next = (
        from_behind(grad_keys[:, :WINDOW].astype(jnp.bfloat16), "seq", -1).astype(jnp.float32),
        from_behind(grad_values[:, :WINDOW].astype(jnp.bfloat16), "seq", -1).astype(jnp.float32),
    )
    grad_key_own = grad_keys[:, WINDOW:] + grad_key_next
    grad_value_own = grad_values[:, WINDOW:] + grad_value_next
    head_back = jax.vjp(
        partial(head_post, cos_table=cos_table, sine_table=sine_table),
        project,
        gain_query,
        gain_key,
    )[1]
    grad_project, grad_gain_query, grad_gain_key = head_back(
        (grad_queries, grad_key_own, grad_value_own)
    )
    grad_project_low = grad_project.reshape(row_count, -1).astype(jnp.bfloat16)
    grad_project_low, ffn_sum = together(grad_project_low, ffn_sum)
    ffn_sum = advance(ffn_steps, ffn_sum)
    grad_normed = jnp.einsum(
        "nk,dk->nd", grad_project_low, w_qkv, preferred_element_type=jnp.float32
    )
    in_back = jax.vjp(rms_scale, tokens, gain_in)[1]
    grad_tokens, grad_gain_in = in_back(grad_normed)
    input_grad = (
        (grad_middle + grad_tokens).astype(jnp.bfloat16).reshape(seqs_here, span_rows, model_width)
    )
    grad_gains = jnp.concatenate(
        [
            grad_gain_in,
            grad_gain_attn,
            grad_gain_pre,
            grad_gain_post,
            grad_gain_query,
            grad_gain_key,
        ]
    )
    qkv_here = qkv_weight.shape[1]
    gains_here = norm_gains.shape[0]
    gain_rows = jnp.pad(
        grad_gains.astype(jnp.bfloat16).reshape(shards, gains_here // 128, 128),
        ((0, 0), (0, 64 - gains_here // 128), (0, model_width - 128)),
    )
    qkv_parts = low_dot("nd,nk->dk", normed, grad_project_low).astype(jnp.bfloat16)
    qkv_parts = qkv_parts.reshape(model_width, shards, -1).swapaxes(0, 1)
    attn_parts = jnp.concatenate(
        [jnp.concatenate([qkv_parts, out_parts], axis=2), gain_rows], axis=1
    )
    attn_steps = reduce_steps(attn_parts)
    attn_total = finish(attn_steps, next(attn_steps))
    ffn_total = finish(ffn_steps, ffn_sum)
    masters = (qkv_weight, out_weight, ff_in_weight, ff_out_weight, norm_gains)
    moments = (qkv_moment, out_moment, ff_in_moment, ff_out_moment, gains_moment)
    squares = (qkv_square, out_square, ff_in_square, ff_out_square, gains_square)
    step_rates = (rate_matrix, rate_matrix, rate_matrix, rate_matrix, rate_gain)
    decays = (decay_matrix, decay_matrix, decay_matrix, decay_matrix, 0.0)
    down_total, out_total = turn(
        ffn_total[2 * model_width :], attn_total[:model_width, qkv_here:]
    )
    totals = (
        attn_total[:model_width, :qkv_here].astype(jnp.float32),
        out_total,
        ffn_total[: 2 * model_width].reshape(ff_in_weight.shape).astype(jnp.float32),
        down_total,
        attn_total[model_width : model_width + gains_here // 128, :128]
        .reshape(gains_here)
        .astype(jnp.float32),
    )
    results = [
        adam_step(
            masters[weight_index],
            totals[weight_index],
            moments[weight_index],
            squares[weight_index],
            step_rates[weight_index],
            decays[weight_index],
        )
        for weight_index in range(5)
    ]
    return (
        mixed,
        input_grad,
        results[0][0],
        results[0][1],
        results[0][2],
        results[1][0],
        results[1][1],
        results[1][2],
        results[2][0],
        results[2][1],
        results[2][2],
        results[3][0],
        results[3][1],
        results[3][2],
        results[4][0],
        results[4][1],
        results[4][2],
    )


def solution(mesh):
    return jax.shard_map(
        on_device,
        mesh=mesh,
        in_specs=(
            P("shard", "seq", None),
            P("shard", "seq", None),
            P("shard", "seq"),
            P("shard", "seq"),
            P(None, "shard"),
            P("shard", None),
            P(None, None, "shard"),
            P("shard", None),
            P("shard"),
            P(None, "shard"),
            P(None, "shard"),
            P("shard", None),
            P("shard", None),
            P(None, None, "shard"),
            P(None, None, "shard"),
            P("shard", None),
            P("shard", None),
            P("shard"),
            P("shard"),
        ),
        out_specs=(
            P("shard", "seq", None),
            P("shard", "seq", None),
            P(None, "shard"),
            P(None, "shard"),
            P(None, "shard"),
            P("shard", None),
            P("shard", None),
            P("shard", None),
            P(None, None, "shard"),
            P(None, None, "shard"),
            P(None, None, "shard"),
            P("shard", None),
            P("shard", None),
            P("shard", None),
            P("shard"),
            P("shard"),
            P("shard"),
        ),
        check_vma=False,
    )
```

```python
from functools import partial

import jax
import jax.numpy as jnp
from jax import lax
from jax.experimental import pallas as pl
from jax.experimental.pallas import tpu as pltpu
from jax.sharding import PartitionSpec as P

D = 640
QH = 4
HEAD = 256
WINDOW = 512
STEP = 10


eps_norm = 1e-06
rope_base = 10000.0
beta_first = 0.9
beta_second = 0.95
adam_eps = 1e-08
rate_matrix = 0.05
rate_gain = 0.8
decay_matrix = 0.1
masked_score = -1e30


def from_behind(block, axis, distance):
    devices = range(lax.axis_size(axis))
    route = [(i - distance, i) for i in devices if i - distance in devices]
    return lax.ppermute(block, axis, route)


def swap_bit(block, axis, bit):
    return lax.ppermute(block, axis, [(i, i ^ (1 << bit)) for i in range(lax.axis_size(axis))])


def my_bit(axis, bit):
    return (lax.axis_index(axis) >> bit) & 1


def halve(block, axis, bit, at):
    mine = my_bit(axis, bit)
    sent = lax.dynamic_index_in_dim(block, 1 - mine, at, keepdims=False)
    kept = lax.dynamic_index_in_dim(block, mine, at, keepdims=False)
    came = swap_bit(sent, axis, bit)
    return (kept.astype(jnp.float32) + came.astype(jnp.float32)).astype(jnp.bfloat16)


def bits_of(axis):
    return lax.axis_size(axis).bit_length() - 1


def reduce_steps(block):
    for bit in range(bits_of("shard")):
        block = halve(block.reshape((-1, 2) + block.shape[1:]), "shard", bit, 1)
        block = yield block
    yield from seq_steps(block[0])


def seq_steps(block):
    for bit in range(bits_of("seq")):
        block = halve(block.reshape((2, -1) + block.shape[1:]), "seq", bit, 0)
        block = yield block
    for bit in reversed(range(bits_of("seq"))):
        came = swap_bit(block, "seq", bit)
        low = my_bit("seq", bit) == 0
        block = jnp.concatenate([jnp.where(low, block, came), jnp.where(low, came, block)], axis=0)
        block = yield block


def advance(steps, block):
    try:
        return steps.send(block)
    except StopIteration:
        return block


def finish(steps, block):
    while True:
        try:
            block = steps.send(block)
        except StopIteration:
            return block


def together(*values):
    return lax.optimization_barrier(values)


def rms_scale(values, scales):
    return values * lax.rsqrt(jnp.mean(values * values, axis=-1, keepdims=True) + eps_norm) * scales


def rope_tables(positions):
    freqs = 1.0 / rope_base ** (jnp.arange(0, HEAD, 2, dtype=jnp.float32) / HEAD)
    angles = positions.astype(jnp.float32)[..., None] * freqs
    return (jnp.cos(angles), jnp.sin(angles))


def rotate(values, cos_table, sine_table):
    half_width = values.shape[-1] // 2
    first_half = values[..., :half_width]
    second_half = values[..., half_width:]
    return jnp.concatenate(
        [
            first_half * cos_table - second_half * sine_table,
            second_half * cos_table + first_half * sine_table,
        ],
        axis=-1,
    )


def split_gains(gain_all):
    return (
        gain_all[0:D],
        gain_all[D : 2 * D],
        gain_all[2 * D : 3 * D],
        gain_all[3 * D : 4 * D],
        gain_all[4 * D : 4 * D + HEAD],
        gain_all[4 * D + HEAD : 4 * D + 2 * HEAD],
    )


def head_post(pieces, gain_query, gain_key, cos_table, sine_table):
    queries = [rotate(rms_scale(p, gain_query), cos_table, sine_table) for p in pieces[:QH]]
    key_rows = rotate(rms_scale(pieces[QH], gain_key), cos_table, sine_table)
    return (queries, key_rows, pieces[QH + 1])


f32 = jnp.float32
bf16 = jnp.bfloat16
row_block = 256
vmem_most = 56 * 1024 * 1024


def dot_nn(a, b):
    return lax.dot_general(a, b, (((1,), (0,)), ((), ())), preferred_element_type=f32)


def dot_nt(a, b):
    return lax.dot_general(a, b, (((1,), (1,)), ((), ())), preferred_element_type=f32)


def inverse_rms(v):
    return lax.rsqrt(jnp.mean(v * v, axis=-1, keepdims=True) + eps_norm)


def rms_back(v, r, gain, dy):
    gdy = gain * dy
    return r * gdy - v * (r * r * r) * jnp.mean(gdy * v, axis=-1, keepdims=True)


def window_probs(block, head, q_ref, k_ref, seg_q_ref, seg_k_ref):
    rows = slice(block * row_block, (block + 1) * row_block)
    reach = slice(block * row_block, (block + 1) * row_block + WINDOW)
    query = q_ref[0, rows, head * HEAD : (head + 1) * HEAD]
    shape = (row_block, row_block + WINDOW)
    ahead = lax.broadcasted_iota(jnp.int32, shape, 1) - lax.broadcasted_iota(jnp.int32, shape, 0)
    same = seg_q_ref[0, rows] == seg_k_ref[0, :, reach]
    allowed = (ahead > 0) & (ahead <= WINDOW) & same
    scores = dot_nt(query, k_ref[0, reach]) * HEAD ** (-0.5)
    scores = jnp.where(allowed, scores, masked_score)
    terms = jnp.exp(scores - jnp.max(scores, axis=-1, keepdims=True))
    return query, terms * (1.0 / jnp.sum(terms, axis=-1, keepdims=True))


def attend_kernel(blocks, q_ref, k_ref, v_ref, seg_q_ref, seg_k_ref, o_ref):
    for block in range(blocks):
        rows = slice(block * row_block, (block + 1) * row_block)
        reach = slice(block * row_block, (block + 1) * row_block + WINDOW)
        for head in range(QH):
            _, probs = window_probs(block, head, q_ref, k_ref, seg_q_ref, seg_k_ref)
            out = dot_nn(probs.astype(bf16), v_ref[0, reach])
            o_ref[0, rows, head * HEAD : (head + 1) * HEAD] = out.astype(bf16)


def attend_back_kernel(
    blocks, q_ref, k_ref, v_ref, seg_q_ref, seg_k_ref, do_ref, dq_ref, dk_ref, dv_ref
):
    dk_ref[...] = jnp.zeros_like(dk_ref)
    dv_ref[...] = jnp.zeros_like(dv_ref)
    for block in range(blocks):
        rows = slice(block * row_block, (block + 1) * row_block)
        reach = slice(block * row_block, (block + 1) * row_block + WINDOW)
        for head in range(QH):
            cols = slice(head * HEAD, (head + 1) * HEAD)
            query, probs = window_probs(block, head, q_ref, k_ref, seg_q_ref, seg_k_ref)
            do = do_ref[0, rows, cols]
            dprobs = dot_nt(do, v_ref[0, reach])
            inner = jnp.sum(probs * dprobs, axis=-1, keepdims=True)
            dscores = (probs * (dprobs - inner)).astype(bf16)
            dq_ref[0, rows, cols] = dot_nn(dscores, k_ref[0, reach]) * HEAD ** (-0.5)
            dk_ref[0, reach] += dot_nn(dscores.T, query) * HEAD ** (-0.5)
            dv_ref[0, reach] += dot_nn(probs.astype(bf16).T, do)


def one_sequence(array):
    return pl.BlockSpec((1,) + array.shape[1:], lambda i: (i,) + (0,) * (len(array.shape) - 1))


def attention_call(kernel, operands, outs, flops, name):
    seqs, span = operands[0].shape[:2]
    return pl.pallas_call(
        partial(kernel, span // row_block),
        grid=(seqs,),
        in_specs=[one_sequence(operand) for operand in operands],
        out_specs=[one_sequence(out) for out in outs],
        out_shape=outs,
        compiler_params=pltpu.CompilerParams(vmem_limit_bytes=40 * 1024 * 1024),
        cost_estimate=pl.CostEstimate(
            flops=flops, bytes_accessed=16 << 20, transcendentals=seqs * span * 4 * 768
        ),
        name=name,
    )(*operands)


def middle_kernel(
    blocks, shards,
    x_ref, o_ref, e_ref, w_out_ref, w_0_ref, w_1_ref, w_2_ref, w_3_ref, gains_ref,
    mixed_ref, dx2_ref, do_ref, keep_ref, send_ref, out_ref, dgains_ref,
    act, slope, h2_all, dm_all, db_all, o_all, hid_all, dg_all, du_all,
):
    step = pl.program_id(0)
    weights = (w_0_ref, w_1_ref, w_2_ref, w_3_ref)
    ff = w_0_ref.shape[2]
    model = x_ref.shape[1]
    heads = out_ref.shape[2]

    @pl.when(step < blocks)
    def _():
        rows = pl.ds(pl.multiple_of(step * row_block, row_block), row_block)
        gain_attn, gain_pre, gain_post = gains_ref[0:1], gains_ref[1:2], gains_ref[2:3]
        x = x_ref[...].astype(f32)
        e = e_ref[...].astype(f32)
        o = o_ref[...]
        branch = dot_nn(o, w_out_ref[...])
        r_branch = inverse_rms(branch)
        x2 = x + branch * r_branch * gain_attn
        r_x2 = inverse_rms(x2)
        h2 = (x2 * r_x2 * gain_pre).astype(bf16)
        m = jnp.zeros((row_block, model), f32)
        for s in range(shards):
            cols = slice(s * ff, (s + 1) * ff)
            gate = dot_nn(h2, weights[s][0])
            up = dot_nn(h2, weights[s][1])
            c = (2.0 / jnp.pi) ** 0.5
            sq = gate * gate
            t = jnp.tanh(c * gate * (1.0 + 0.044715 * sq))
            half = 0.5 * (1.0 + t)
            gelu = gate * half
            act[:, cols] = gelu
            slope[:, cols] = up * (
                half + 0.5 * gate * (1.0 - t * t) * (c * (1.0 + 3 * 0.044715 * sq))
            )
            hidden = (gelu * up).astype(bf16)
            hid_all[s, rows] = hidden
            m += dot_nt(hidden, weights[s][2])
        r_m = inverse_rms(m)
        mixed_ref[...] = (x2 + m * r_m * gain_post).astype(bf16)
        dm = rms_back(m, r_m, gain_post, e).astype(bf16)
        dh2 = jnp.zeros((row_block, model), f32)
        for s in range(shards):
            cols = slice(s * ff, (s + 1) * ff)
            dh = dot_nn(dm, weights[s][2])
            dgate = (dh * slope[:, cols]).astype(bf16)
            dup = (dh * act[:, cols]).astype(bf16)
            dg_all[s, rows] = dgate
            du_all[s, rows] = dup
            dh2 += dot_nt(dgate, weights[s][0]) + dot_nt(dup, weights[s][1])
        dx2 = e + rms_back(x2, r_x2, gain_pre, dh2)
        dx2_ref[...] = dx2
        db = rms_back(branch, r_branch, gain_attn, dx2).astype(bf16)
        do_ref[...] = dot_nt(db, w_out_ref[...]).astype(bf16)
        h2_all[rows] = h2
        dm_all[rows] = dm
        db_all[rows] = db
        for s in range(shards):
            o_all[s, rows] = o[:, s * heads : (s + 1) * heads]

        @pl.when(step == 0)
        def _():
            dgains_ref[...] = jnp.zeros_like(dgains_ref)

        dgains_ref[0:1] += jnp.sum(dx2 * branch * r_branch, axis=0, keepdims=True)
        dgains_ref[1:2] += jnp.sum(dh2 * x2 * r_x2, axis=0, keepdims=True)
        dgains_ref[2:3] += jnp.sum(e * m * r_m, axis=0, keepdims=True)

    @pl.when(step >= blocks)
    def _():
        turn_at = step - blocks
        piece = lax.rem(turn_at + shards // 2, shards)
        h2_t = h2_all[...].T
        gate = dot_nn(h2_t, dg_all[piece]).astype(bf16)
        up = dot_nn(h2_t, du_all[piece]).astype(bf16)
        down = dot_nn(dm_all[...].T, hid_all[piece]).astype(bf16)
        out_ref[0] = dot_nn(db_all[...].T, o_all[turn_at]).astype(bf16)

        @pl.when(turn_at < shards // 2)
        def _():
            send_ref[0, 0:model] = gate
            send_ref[0, model : 2 * model] = up
            send_ref[0, 2 * model : 3 * model] = down

        @pl.when(turn_at >= shards // 2)
        def _():
            keep_ref[0, 0:model] = gate
            keep_ref[0, model : 2 * model] = up
            keep_ref[0, 2 * model : 3 * model] = down


def middle(x, attended, out_grad, w_out, weights, gains):
    rows, model = x.shape
    inner = attended.shape[1]
    shards, ff = len(weights), weights[0].shape[2]
    half = shards // 2
    blocks = rows // row_block
    heads = inner // shards

    def row_spec(width):
        return pl.BlockSpec((row_block, width), lambda i: (jnp.minimum(i, blocks - 1), 0))

    def whole(shape):
        return pl.BlockSpec(shape, lambda i: (0,) * len(shape), pipeline_mode=pl.Buffered(1))

    def shard_spec(shape, first, count):
        return pl.BlockSpec(
            (1,) + shape, lambda i: (jnp.clip(i - blocks - first, 0, count - 1), 0, 0)
        )

    return pl.pallas_call(
        partial(middle_kernel, blocks, shards),
        grid=(blocks + shards,),
        in_specs=[
            row_spec(model), row_spec(inner), row_spec(model),
            whole(w_out.shape), *[whole(weight.shape) for weight in weights], whole(gains.shape),
        ],
        out_specs=[
            row_spec(model), row_spec(model), row_spec(inner),
            shard_spec((3 * model, ff), half, half), shard_spec((3 * model, ff), 0, half),
            shard_spec((model, heads), 0, shards),
            pl.BlockSpec((8, model), lambda i: (0, 0)),
        ],
        out_shape=[
            jax.ShapeDtypeStruct((rows, model), bf16),
            jax.ShapeDtypeStruct((rows, model), f32),
            jax.ShapeDtypeStruct((rows, inner), bf16),
            jax.ShapeDtypeStruct((half, 3 * model, ff), bf16),
            jax.ShapeDtypeStruct((half, 3 * model, ff), bf16),
            jax.ShapeDtypeStruct((shards, model, heads), bf16),
            jax.ShapeDtypeStruct((8, model), f32),
        ],
        scratch_shapes=[
            pltpu.VMEM((row_block, shards * ff), f32),
            pltpu.VMEM((row_block, shards * ff), f32),
            pltpu.VMEM((rows, model), bf16),
            pltpu.VMEM((rows, model), bf16),
            pltpu.VMEM((rows, model), bf16),
            pltpu.VMEM((shards, rows, heads), bf16),
            pltpu.VMEM((shards, rows, ff), bf16),
            pltpu.VMEM((shards, rows, ff), bf16),
            pltpu.VMEM((shards, rows, ff), bf16),
        ],
        compiler_params=pltpu.CompilerParams(vmem_limit_bytes=vmem_most),
        cost_estimate=pl.CostEstimate(
            flops=2 * rows * model * 3 * (3 * shards * ff + inner),
            bytes_accessed=30 << 20, transcendentals=rows * shards * ff,
        ),
        name="middle",
    )(x, attended, out_grad, w_out, *weights, gains)


def turn_kernel(ffn_ref, attn_ref, down_ref, out_ref):
    down_ref[...] = ffn_ref[...].astype(f32).T
    out_ref[...] = attn_ref[...].astype(f32).T


def turn(ffn_part, attn_part):
    return pl.pallas_call(
        turn_kernel,
        out_shape=[
            jax.ShapeDtypeStruct(part.shape[::-1], f32) for part in (ffn_part, attn_part)
        ],
        compiler_params=pltpu.CompilerParams(vmem_limit_bytes=24 * 1024 * 1024),
        name="turn",
    )(ffn_part, attn_part)


def adam_step(weight, gradient, moment, square, step_rate, decay_rate):
    moment_new = beta_first * moment + (1.0 - beta_first) * gradient
    square_new = beta_second * square + (1.0 - beta_second) * gradient * gradient
    moment_hat = moment_new / (1.0 - beta_first**STEP)
    square_hat = square_new / (1.0 - beta_second**STEP)
    weight_new = weight - step_rate * (
        moment_hat / (jnp.sqrt(square_hat) + adam_eps) + decay_rate * weight
    )
    return (weight_new, moment_new, square_new)


def on_device(
    block_input,
    out_grad,
    positions,
    segments,
    qkv_weight,
    out_weight,
    ff_in_weight,
    ff_out_weight,
    norm_gains,
    qkv_moment,
    qkv_square,
    out_moment,
    out_square,
    ff_in_moment,
    ff_in_square,
    ff_out_moment,
    ff_out_square,
    gains_moment,
    gains_square,
):
    seqs_here, span_rows, model_width = block_input.shape
    row_count = seqs_here * span_rows
    w_qkv, w_out, gains_low = (
        lax.all_gather(qkv_weight.astype(jnp.bfloat16), "shard", axis=1, tiled=True),
        lax.all_gather(out_weight.astype(jnp.bfloat16), "shard", axis=0, tiled=True),
        lax.all_gather(norm_gains.astype(jnp.bfloat16), "shard", axis=0, tiled=True),
    )
    gain_in, gain_attn, gain_pre, gain_post, gain_query, gain_key = split_gains(
        gains_low.astype(jnp.float32)
    )
    tokens = block_input.astype(jnp.float32).reshape(row_count, model_width)
    normed = rms_scale(tokens, gain_in).astype(jnp.bfloat16)
    ffn_own = jnp.concatenate(
        [ff_in_weight.astype(jnp.bfloat16), ff_out_weight.astype(jnp.bfloat16).T[None]], axis=0
    )
    ffn_own, w_qkv = together(ffn_own, w_qkv)
    ffn_x = swap_bit(ffn_own, "shard", 1)
    ffn_core = swap_bit(ffn_own, "shard", 0)
    ffn_both = swap_bit(ffn_x, "shard", 0)
    project = jnp.dot(normed, w_qkv, preferred_element_type=jnp.float32).reshape(
        seqs_here, span_rows, -1
    )
    pieces = [project[..., i * HEAD : (i + 1) * HEAD] for i in range(QH + 2)]
    cos_table, sine_table = rope_tables(positions)
    query_full, key_full, value_full = head_post(
        pieces, gain_query, gain_key, cos_table, sine_table
    )
    queries = jnp.concatenate([part.astype(jnp.bfloat16) for part in query_full], axis=-1)
    keys_own = key_full.astype(jnp.bfloat16)
    values_own = value_full.astype(jnp.bfloat16)
    key_prev, value_prev, segment_prev = from_behind((keys_own, values_own, segments), "seq", 1)
    is_first = lax.axis_index("seq") == 0
    key_segments = jnp.concatenate([jnp.where(is_first, -1, segment_prev), segments], axis=1)
    all_keys = jnp.concatenate([key_prev, keys_own], axis=1)
    all_values = jnp.concatenate([value_prev, values_own], axis=1)
    operands = (queries, all_keys, all_values, segments[:, :, None], key_segments[:, None, :])
    attention_flops = 2 * 2 * row_count * QH * (WINDOW + row_block) * HEAD
    (attended_low,) = attention_call(
        attend_kernel,
        operands,
        [jax.ShapeDtypeStruct(queries.shape, jnp.bfloat16)],
        attention_flops,
        "attend",
    )
    attended_low = attended_low.reshape(row_count, QH * HEAD)
    shards = lax.axis_size("shard")
    low_dot = partial(jnp.einsum, preferred_element_type=jnp.float32)
    mixed, grad_middle, grad_attended, ffn_keep, ffn_send, out_parts, grad_three = middle(
        block_input.reshape(row_count, model_width),
        attended_low,
        out_grad.reshape(row_count, model_width),
        w_out,
        (ffn_own, ffn_x, ffn_core, ffn_both),
        jnp.stack([gain_attn, gain_pre, gain_post]),
    )
    mixed = mixed.reshape(block_input.shape)
    grad_gain_attn, grad_gain_pre, grad_gain_post = grad_three[0], grad_three[1], grad_three[2]
    ffn_came = swap_bit(ffn_send, "shard", 0)
    grad_queries, grad_keys, grad_values = attention_call(
        attend_back_kernel,
        operands + (grad_attended.reshape(queries.shape),),
        [
            jax.ShapeDtypeStruct(queries.shape, jnp.float32),
            jax.ShapeDtypeStruct(all_keys.shape, jnp.float32),
            jax.ShapeDtypeStruct(all_keys.shape, jnp.float32),
        ],
        attention_flops * 5 // 2,
        "attend_back",
    )
    grad_queries, ffn_came = together(grad_queries, ffn_came)
    ffn_pair = ffn_keep.astype(jnp.float32) + ffn_came.astype(jnp.float32)
    ffn_came = swap_bit(ffn_pair[1].astype(jnp.bfloat16), "shard", 1)
    grad_key_next, grad_value_next = (
        from_behind(grad_keys[:, :WINDOW].astype(jnp.bfloat16), "seq", -1).astype(jnp.float32),
        from_behind(grad_values[:, :WINDOW].astype(jnp.bfloat16), "seq", -1).astype(jnp.float32),
    )
    grad_key_own = grad_keys[:, WINDOW:] + grad_key_next
    grad_value_own = grad_values[:, WINDOW:] + grad_value_next
    head_back = jax.vjp(
        partial(head_post, cos_table=cos_table, sine_table=sine_table),
        pieces,
        gain_query,
        gain_key,
    )[1]
    grad_pieces, grad_gain_query, grad_gain_key = head_back(
        (
            [grad_queries[..., i * HEAD : (i + 1) * HEAD] for i in range(QH)],
            grad_key_own,
            grad_value_own,
        )
    )
    grad_project_low = jnp.concatenate(
        [piece.astype(jnp.bfloat16) for piece in grad_pieces], axis=-1
    ).reshape(row_count, -1)
    grad_project_low, ffn_came = together(grad_project_low, ffn_came)
    ffn_steps = seq_steps((ffn_pair[0] + ffn_came.astype(jnp.float32)).astype(jnp.bfloat16))
    ffn_sum = next(ffn_steps)
    grad_normed = jnp.einsum(
        "nk,dk->nd", grad_project_low, w_qkv, preferred_element_type=jnp.float32
    )
    in_back = jax.vjp(rms_scale, tokens, gain_in)[1]
    grad_tokens, grad_gain_in = in_back(grad_normed)
    input_grad = (
        (grad_middle + grad_tokens).astype(jnp.bfloat16).reshape(seqs_here, span_rows, model_width)
    )
    grad_gains = jnp.concatenate(
        [
            grad_gain_in,
            grad_gain_attn,
            grad_gain_pre,
            grad_gain_post,
            grad_gain_query,
            grad_gain_key,
        ]
    )
    qkv_here = qkv_weight.shape[1]
    gains_here = norm_gains.shape[0]
    gain_rows = jnp.pad(
        grad_gains.astype(jnp.bfloat16).reshape(shards, gains_here // 128, 128),
        ((0, 0), (0, 64 - gains_here // 128), (0, model_width - 128)),
    )
    qkv_parts = low_dot("nd,nk->dk", normed, grad_project_low).astype(jnp.bfloat16)
    qkv_parts = qkv_parts.reshape(model_width, shards, -1).swapaxes(0, 1)
    attn_parts = jnp.concatenate(
        [jnp.concatenate([qkv_parts, out_parts], axis=2), gain_rows], axis=1
    )
    attn_steps = reduce_steps(attn_parts)
    attn_total = finish(attn_steps, next(attn_steps))
    ffn_total = finish(ffn_steps, ffn_sum)
    masters = (qkv_weight, out_weight, ff_in_weight, ff_out_weight, norm_gains)
    moments = (qkv_moment, out_moment, ff_in_moment, ff_out_moment, gains_moment)
    squares = (qkv_square, out_square, ff_in_square, ff_out_square, gains_square)
    step_rates = (rate_matrix, rate_matrix, rate_matrix, rate_matrix, rate_gain)
    decays = (decay_matrix, decay_matrix, decay_matrix, decay_matrix, 0.0)
    down_total, out_total = turn(
        ffn_total[2 * model_width :], attn_total[:model_width, qkv_here:]
    )
    totals = (
        attn_total[:model_width, :qkv_here].astype(jnp.float32),
        out_total,
        ffn_total[: 2 * model_width].reshape(ff_in_weight.shape).astype(jnp.float32),
        down_total,
        attn_total[model_width : model_width + gains_here // 128, :128]
        .reshape(gains_here)
        .astype(jnp.float32),
    )
    results = [
        adam_step(
            masters[weight_index],
            totals[weight_index],
            moments[weight_index],
            squares[weight_index],
            step_rates[weight_index],
            decays[weight_index],
        )
        for weight_index in range(5)
    ]
    return (
        mixed,
        input_grad,
        results[0][0],
        results[0][1],
        results[0][2],
        results[1][0],
        results[1][1],
        results[1][2],
        results[2][0],
        results[2][1],
        results[2][2],
        results[3][0],
        results[3][1],
        results[3][2],
        results[4][0],
        results[4][1],
        results[4][2],
    )


def solution(mesh):
    return jax.shard_map(
        on_device,
        mesh=mesh,
        in_specs=(
            P("shard", "seq", None),
            P("shard", "seq", None),
            P("shard", "seq"),
            P("shard", "seq"),
            P(None, "shard"),
            P("shard", None),
            P(None, None, "shard"),
            P("shard", None),
            P("shard"),
            P(None, "shard"),
            P(None, "shard"),
            P("shard", None),
            P("shard", None),
            P(None, None, "shard"),
            P(None, None, "shard"),
            P("shard", None),
            P("shard", None),
            P("shard"),
            P("shard"),
        ),
        out_specs=(
            P("shard", "seq", None),
            P("shard", "seq", None),
            P(None, "shard"),
            P(None, "shard"),
            P(None, "shard"),
            P("shard", None),
            P("shard", None),
            P("shard", None),
            P(None, None, "shard"),
            P(None, None, "shard"),
            P(None, None, "shard"),
            P("shard", None),
            P("shard", None),
            P("shard", None),
            P("shard"),
            P("shard"),
            P("shard"),
        ),
        check_vma=False,
    )
```
